128 devices in a mesh: dp: 16 (over x, y_lo, core), vocab: 8 (over y_hi, z).
Axes of the slice: x: 4, y: 4 (y_hi: 2, y_lo: 2; y = y_hi * 2 + y_lo), z: 4, core: 2. Of those that a mesh axis runs over, the one named last changes fastest.
Arguments:
- hidden: bfloat16 [2048, 3584], P('dp'), may hold values from -256 to 256
- head_weight: bfloat16 [3584, 131072], P(None, ('dp', 'vocab')), may hold values from -0.3125 to 0.3125
- teacher_logits: bfloat16 [2048, 16, 8192], P('dp', None, 'vocab'), may hold values from -80 to 160
- upstream: float32 [2048], replicated, may hold values from 2000 to 20000
Outputs:
- grad_hidden: bfloat16 [2048, 3584], P('dp', 'vocab')
- grad_weight: bfloat16 [3584, 131072], P(None, ('dp', 'vocab'))
- kl_rows: float32 [2048], P('dp')
The draws below stay inside these ranges and needn't reach their ends.
All inputs are finite; a program needn't handle non-finite values.
Results may differ from the reference program's by a relative error of at most 0.018.
Values may be sent and summed in bfloat16 or wider, within the bound.
A program may use at most 192 MiB of HBM per device.

```python
import math
import jax
import jax.numpy as jnp
from jax import lax

D = 3584
VOCAB = 131072
ROWS = 2048
N_DP = 16


def draw_hidden(key, part):
    key = jax.random.fold_in(key, 11)
    key_base = jax.random.fold_in(key, 0)
    return jnp.clip(0.2 * jax.random.normal(key_base, (ROWS, D), jnp.float32), -1.2, 1.2).astype(jnp.bfloat16)


def draw_teacher_logits(key, part):
    key = jax.random.fold_in(key, 23)
    key_noise = jax.random.fold_in(key, 0)
    width = VOCAB // N_DP
    shape = (ROWS, N_DP, width)
    return jnp.clip(jax.random.normal(key_noise, shape, jnp.float32), -6.0, 6.0).astype(jnp.bfloat16)


def level_of(rng, extent, pieces, low, top_value):
    def one(axis_at, parts):
        steps = jax.random.uniform(jax.random.fold_in(jax.random.fold_in(rng, 6), axis_at), (parts,), jnp.float32, low / len(pieces), top_value / len(pieces))
        return jnp.repeat(jnp.exp(steps), extent[axis_at] // parts).reshape((-1,) + (1,) * (len(extent) - axis_at - 1))

    gain = one(*pieces[0])
    for cut in pieces[1:]:
        gain = gain * one(*cut)
    return gain


def gaussian(stream_key, shape, scale, most, shards=(), kind=jnp.bfloat16):
    array = scale * jax.random.normal(stream_key, shape, jnp.float32)
    if shards:
        array = array * level_of(stream_key, shape, shards, -0.22, 0.18)
    return jnp.clip(array, -most, most).astype(kind)


def setup_inputs(seed: int = 0) -> dict:
    splits = jax.random.split(jax.random.key(seed), 5)
    hidden = draw_hidden(jax.random.fold_in(splits[4], 71), 0)
    head_weight = gaussian(splits[1], (D, VOCAB), (D // 9) ** -0.5, 0.3125, ((1, 128),))
    teacher_logits = draw_teacher_logits(jax.random.fold_in(splits[4], 71), 0)
    upstream = jnp.clip(jnp.exp(jax.random.uniform(splits[3], (ROWS,), jnp.float32, math.log(2000.0), math.log(20000.0))), 2000.0, 20000.0)
    return dict(hidden=hidden, head_weight=head_weight, teacher_logits=teacher_logits, upstream=upstream)


def reference(hidden, head_weight, teacher_logits, upstream):
    teacher_all = teacher_logits.reshape(ROWS, VOCAB)
    width = VOCAB // N_DP
    blocks = jnp.arange(N_DP, dtype=jnp.int32)

    def logits_of(index):
        start = (index * width).astype(jnp.int32)
        weight_block = lax.dynamic_slice_in_dim(head_weight, start, width, 1)
        student = jnp.dot(hidden, weight_block, preferred_element_type=jnp.float32)
        teacher = lax.dynamic_slice_in_dim(teacher_all, start, width, 1).astype(jnp.float32)
        return weight_block, student, teacher

    def first_pass(carry, index):
        peak_s, total_s, peak_t, total_t, cross = carry
        weight_block, student, teacher = logits_of(index)
        new_s = jnp.maximum(peak_s, jnp.max(student, axis=1))
        new_t = jnp.maximum(peak_t, jnp.max(teacher, axis=1))
        total_s = total_s * jnp.exp(peak_s - new_s) + jnp.sum(jnp.exp(student - new_s[:, None]), axis=1)
        expo_t = jnp.exp(teacher - new_t[:, None])
        factor = jnp.exp(peak_t - new_t)
        total_t = total_t * factor + jnp.sum(expo_t, axis=1)
        cross = cross * factor + jnp.sum(expo_t * (teacher - student), axis=1)
        return (new_s, total_s, new_t, total_t, cross), None

    start_carry = (jnp.full((ROWS,), -jnp.inf, jnp.float32), jnp.zeros((ROWS,), jnp.float32),
                   jnp.full((ROWS,), -jnp.inf, jnp.float32), jnp.zeros((ROWS,), jnp.float32),
                   jnp.zeros((ROWS,), jnp.float32))
    (peak_s, total_s, peak_t, total_t, cross), unused = lax.scan(first_pass, start_carry, blocks)
    lse_s = peak_s + jnp.log(total_s)
    lse_t = peak_t + jnp.log(total_t)
    kl_rows = cross / total_t - lse_t + lse_s

    def second_pass(grad_sum, index):
        weight_block, student, teacher = logits_of(index)
        grad_logits = (upstream[:, None] * (jnp.exp(student - lse_s[:, None]) - jnp.exp(teacher - lse_t[:, None]))).astype(jnp.bfloat16)
        weight_grad = lax.dot_general(hidden, grad_logits, (((0,), (0,)), ((), ())), preferred_element_type=jnp.float32)
        grad_sum = grad_sum + lax.dot_general(grad_logits, weight_block, (((1,), (1,)), ((), ())), preferred_element_type=jnp.float32)
        return grad_sum, weight_grad.astype(jnp.bfloat16)

    grad_sum, weight_blocks = lax.scan(second_pass, jnp.zeros((ROWS, D), jnp.float32), blocks)
    grad_weight = jnp.transpose(weight_blocks, (1, 0, 2)).reshape(D, VOCAB)
    return grad_sum.astype(jnp.bfloat16), grad_weight, kl_rows
```

```python
import jax
import jax.numpy as jnp
from jax import lax
from jax.experimental import pallas as pl
from jax.experimental.pallas import tpu as pltpu
from jax.sharding import PartitionSpec as P

D = 3584
F = 448
C = 1024
BF = jnp.bfloat16
F32 = jnp.float32
MESH = pl.DeviceIdType.MESH
ORDERS = ((0, 1, 2), (1, 2, 0), (2, 0, 1))
START = (0, 160, 304)
COUNT = (160, 144, 144)
HALF = 80


def m4(a):
    return (a + 8) % 4


def dot(a, b, dims):
    return lax.dot_general(a, b, (dims, ((), ())), preferred_element_type=F32)


def kernel(hid, w, t2, up, gh_out, gw_out, kl_out, H, HO, W2, T, S, GX, SB, RA0, RA1, RA2, RB0, RB1, RB2, RC0, RC1, RC2,
           RD, PM, PS, ST, SR, CT, CR, LSE, FIN, stage, s_loc, s_x, s_y0, s_y, s_z, s_f, s_a, s_w, s_h, s_g, s_st, s_ct,
           s_rb, s_ra, s_rc, s_rd, s_out):
    d = lax.axis_index("dp")
    v = lax.axis_index("vocab")
    x = d // 4
    p = (d // 2) % 2
    c = d % 2
    yh = v // 4
    y = yh * 2 + p
    z = v % 4
    me = (x, y, z)

    def dev(xx, yy, zz, cc):
        return (xx * 4 + (yy % 2) * 2 + cc, (yy // 2) * 4 + zz)

    def along(axis, k):
        at = [x, y, z]
        at[axis] = m4(at[axis] + k)
        return dev(*at, c)

    sibling = dev(x, y, z, 1 - c)
    yn = m4(y - 1 + 2 * p)
    yl = y + 1 - 2 * p
    dyn = dev(x, yn, z, c)
    xt = [m4(x + 1), m4(x - 1), m4(x + 2)]
    xq = [m4(x - 1), m4(x + 1), m4(x + 2)]
    dz = [along(2, 1), along(2, -1)]
    zq = [m4(z - 1), m4(z + 1)]
    a2a = [(xt[0], yl), (xt[2], y), (xt[1], y), (xt[0], y), (x, yl), (xt[2], yl), (xt[1], yl)]
    a2s = [(xq[0], yl), (xq[2], y), (xq[1], y), (xq[0], y), (x, yl), (xq[2], yl), (xq[1], yl)]
    da = [dev(a, b, z, c) for a, b in a2a]

    partners = [along(a, k) for a in range(3) for k in (1, 2, 3)] + [sibling, da[0], da[5], da[6]]
    barrier = pltpu.get_barrier_semaphore()
    for to in partners:
        pl.semaphore_signal(barrier, inc=1, device_id=to, device_id_type=MESH)
    pl.semaphore_wait(barrier, len(partners))

    def send(src, dst, sems, at, to):
        return pltpu.make_async_remote_copy(
            src_ref=src, dst_ref=dst, send_sem=sems.at[(0, *at)], recv_sem=sems.at[(1, *at)],
            device_id=to, device_id_type=MESH)

    own = pl.ds(pl.multiple_of(z * 32, 32), 32)
    X = [send(hid.at[own], H.at[x, p, z], s_x, (i,), along(0, (1, -1, 2)[i])) for i in range(3)]
    A = [send(t2.at[:, pl.ds(pl.multiple_of((a * 2 + b % 2) * 2 * C, 2 * C), 2 * C)], T.at[x * 2 + p], s_a, (k,), da[k])
         for k, (a, b) in enumerate(a2a)]
    Y0 = [send(hid.at[pl.ds(pl.multiple_of(m4(z + k) * 32, 32), 32)], H.at[x, p, m4(z + k)], s_y0, (k,), dyn)
          for k in range(4)]
    Y1 = [send(H.at[xq[i], p, z], H.at[xq[i], p, z], s_y, (i,), dyn) for i in range(3)]
    Z = [[[send(H.at[xq[i], (p + q) % 2, z], H.at[xq[i], (p + q) % 2, z], s_z, (i, q, r), dz[r])
           for r in range(2)] for q in range(2)] for i in range(3)]
    FW = [[[send(H.at[xq[i], (p + q) % 2, zq[r], pl.ds(16 * r, 16)], H.at[xq[i], (p + q) % 2, zq[r], pl.ds(16 * r, 16)],
                 s_f, (i, q, r), dz[r]) for r in range(2)] for q in range(2)] for i in range(3)]
    WC = send(w, W2.at[c], s_w, (), sibling)
    local = [pltpu.make_async_copy(hid.at[pl.ds(32 * k, 32)], H.at[x, p, k], s_loc.at[k]) for k in range(4)]
    local.append(pltpu.make_async_copy(w, W2.at[c], s_loc.at[4]))
    local.append(pltpu.make_async_copy(
        t2.at[:, pl.ds(pl.multiple_of((x * 2 + p) * 2 * C, 2 * C), 2 * C)], T.at[x * 2 + p], s_loc.at[5]))
    for i in range(3):
        X[i].start()
    Y0[0].start()
    for k in range(7):
        A[k].start()
    WC.start()
    for l in local:
        l.start()
    for i in range(3):
        X[i].wait_recv()
        Y1[i].start()
        Z[i][0][0].start()
        Z[i][0][1].start()
    for k in range(1, 4):
        Y0[k].start()
    for i in range(3):
        Y1[i].wait_recv()
        Z[i][1][0].start()
        Z[i][1][1].start()
    for l in local:
        l.wait()
    Y0[0].wait_recv()
    WC.wait_recv()

    def student(zz):
        def tile(n, carry):
            j = (n // 4 + c) % 2
            k = pl.multiple_of((n % 4) * 256, 256)
            rows = H[:, :, zz].reshape(256, D)
            out = jnp.dot(rows, W2[j, :, pl.ds(k, 256)], preferred_element_type=F32)
            S[:, :, zz, :, pl.ds(pl.multiple_of(j * C + k, 256), 256)] = out.reshape(4, 2, 32, 256)
            return carry

        lax.fori_loop(0, 8, tile, 0)

        def stats(b, carry):
            xx, pp = b // 2, b % 2
            top = S[xx, pp, zz, :, 0:128]
            for g in range(1, 16):
                top = jnp.maximum(top, S[xx, pp, zz, :, g * 128:(g + 1) * 128])
            total = jnp.zeros((32, 128), F32)
            for g in range(16):
                total = total + jnp.exp(S[xx, pp, zz, :, g * 128:(g + 1) * 128] - top)
            PM[xx, pp, zz] = top
            PS[xx, pp, zz] = total
            return carry

        lax.fori_loop(0, 8, stats, 0)

    HX = [send(H.at[:, :, zz], HO.at[:, :, zz], s_h, (k,), sibling) for k, zz in enumerate((z, zq[0], zq[1], m4(z + 2)))]
    HX[0].start()
    student(z)
    for q in range(2):
        for i in range(3):
            for r in range(2):
                Z[i][q][r].wait_recv()
                FW[i][q][r].start()
    for k in range(1, 4):
        Y0[k].wait_recv()
    for r in range(2):
        HX[1 + r].start()
        student(zq[r])

    def merge(top, total):
        top, total = top.T, total.T
        peak = jnp.max(top, axis=0, keepdims=True)
        return peak, jnp.sum(total * jnp.exp(top - peak), axis=0, keepdims=True)

    def teacher(b):
        def part(i, carry):
            rows = pl.ds(pl.multiple_of(i * 32, 32), 32)
            top = T[b, rows, 0:128].astype(F32)
            for g in range(1, 16):
                top = jnp.maximum(top, T[b, rows, g * 128:(g + 1) * 128].astype(F32))
            total = jnp.zeros((32, 128), F32)
            for g in range(16):
                total = total + jnp.exp(T[b, rows, g * 128:(g + 1) * 128].astype(F32) - top)
            FIN[0, rows] = top
            FIN[1, rows] = total
            return carry

        lax.fori_loop(0, 4, part, 0)
        peak, total = merge(FIN[0], FIN[1])
        ST[0, 2, pl.ds(b, 1), :] = peak
        ST[0, 3, pl.ds(b, 1), :] = total

    teacher(x * 2 + p)
    for k in range(7):
        A[k].wait_recv()
        teacher(a2s[k][0] * 2 + a2s[k][1] % 2)
    for q in range(2):
        for i in range(3):
            for r in range(2):
                FW[i][q][r].wait_recv()
    HX[3].start()
    student(m4(z + 2))

    def merge_student(b, carry):
        xx, pp = b // 2, b % 2
        peak, total = merge(PM[xx, pp].reshape(128, 128), PS[xx, pp].reshape(128, 128))
        ST[0, 0, pl.ds(b, 1), :] = peak
        ST[0, 1, pl.ds(b, 1), :] = total
        return carry

    lax.fori_loop(0, 8, merge_student, 0)

    for a in range(3):
        ex = [send(ST.at[a], SR.at[a, k], s_st, (a, k), along(a, k + 1)) for k in range(3)]
        for e in ex:
            e.start()
        for e in ex:
            e.wait()
        for s in range(2):
            tops = [ST[a, 2 * s]] + [SR[a, k, 2 * s] for k in range(3)]
            sums = [ST[a, 2 * s + 1]] + [SR[a, k, 2 * s + 1] for k in range(3)]
            peak = jnp.maximum(jnp.maximum(tops[0], tops[1]), jnp.maximum(tops[2], tops[3]))
            total = sum(u * jnp.exp(t - peak) for t, u in zip(tops, sums))
            ST[a + 1, 2 * s] = peak
            ST[a + 1, 2 * s + 1] = total
    LSE[0] = ST[3, 0] + jnp.log(ST[3, 1])
    LSE[1] = ST[3, 2] + jnp.log(ST[3, 3])

    def grads(b, carry):
        def spread(row):
            return jnp.broadcast_to(row, (128, 128)).T

        FIN[0] = spread(LSE[0, pl.ds(b, 1), :])
        FIN[1] = spread(LSE[1, pl.ds(b, 1), :])
        FIN[2] = spread(up[pl.ds(2 * b + c, 1), :])
        xx, pp = b // 2, b % 2

        def part(i, carry):
            rows = pl.ds(pl.multiple_of(i * 32, 32), 32)
            ls, lt, u = FIN[0, rows], FIN[1, rows], FIN[2, rows]
            cross = jnp.zeros((32, 128), F32)
            for g in range(16):
                at = slice(g * 128, (g + 1) * 128)
                s = S[xx, pp, i, :, at]
                t = T[b, rows, at].astype(F32)
                pt = jnp.exp(t - lt)
                cross = cross + pt * (t - s)
                T[b, rows, at] = (u * (jnp.exp(s - ls) - pt)).astype(BF)
            FIN[3, rows] = cross
            return carry

        lax.fori_loop(0, 4, part, 0)
        CT[0, pl.ds(b, 1), :] = jnp.sum(FIN[3].T, axis=0, keepdims=True)
        return carry

    lax.fori_loop(0, 8, grads, 0)

    GXC = send(T.at[:, :, pl.ds(pl.multiple_of((1 - c) * C, C), C)], GX, s_g, (), sibling)
    GXC.start()
    cex = [[send(CT.at[a], CR.at[a, k], s_ct, (a, k), along(a, k + 1)) for k in range(3)] for a in range(3)]
    for e in cex[0]:
        e.start()

    def unit(xx, hh, zz):
        vv = hh * 4 + zz
        feat = pl.ds(pl.multiple_of(vv * F, 64), F)
        out = dot(W2[0, feat, :], T[pl.ds(2 * xx, 2), :, 0:C].reshape(256, C), ((1,), (1,)))
        out = out + dot(W2[1, feat, :], T[pl.ds(2 * xx, 2), :, C:2 * C].reshape(256, C), ((1,), (1,)))
        out = out.astype(BF)
        SB[xx, 2 * hh, zz] = out[:, 0:128]
        SB[xx, 2 * hh + 1, zz] = out[:, 128:256]

    RA = (RA0, RA1, RA2)
    RB = (RB0, RB1, RB2)
    RC = (RC0, RC1, RC2)

    def at_of(o, coords, rows):
        idx = [slice(None)] * 3
        for axis, a in zip(ORDERS[o], coords):
            if a is not None:
                idx[axis] = a
        return (*idx, rows)

    first = [pl.ds(START[o], HALF) for o in range(3)]
    second = [pl.ds(START[o] + HALF, COUNT[o] - HALF) for o in range(3)]
    whole = [pl.ds(START[o], COUNT[o]) for o in range(3)]
    lo = pl.ds(0, HALF)
    hi = [pl.ds(HALF, COUNT[o] - HALF) for o in range(3)]

    far, relay, near = [], [], []
    for o in range(3):
        ax = ORDERS[o][0]
        a = me[ax]
        plus, minus = along(ax, 1), along(ax, -1)
        far.append([
            send(SB.at[at_of(o, (m4(a + 2),), first[o])], RB[o].at[:, :, lo], s_rb, (o, 0), plus),
            send(SB.at[at_of(o, (m4(a + 2),), second[o])], RB[o].at[:, :, hi[o]], s_rb, (o, 1), minus)])
        near.append([
            send(SB.at[at_of(o, (m4(a + 1),), second[o])], RA[o].at[0, :, :, hi[o]], s_ra, (o, 0), plus),
            send(SB.at[at_of(o, (m4(a - 1),), first[o])], RA[o].at[1, :, :, lo], s_ra, (o, 1), minus)])
        relay.append([
            send(RB[o].at[:, :, lo], RA[o].at[0, :, :, lo], s_ra, (o, 2), plus),
            send(RB[o].at[:, :, hi[o]], RA[o].at[1, :, :, hi[o]], s_ra, (o, 3), minus)])

    def loop(n, f):
        def body(i, carry):
            f(i)
            return carry

        lax.fori_loop(0, n, body, 0)

    loop(8, lambda i: unit(m4(x + 2), i // 4, i % 4))
    for e in far[0]:
        e.start()
    loop(12, lambda i: unit(m4(x + 3 + i // 4), 1 - yh, i % 4))
    for e in far[1]:
        e.start()
    loop(3, lambda i: unit(m4(x + 3 + i), yh, m4(z + 2)))
    for e in far[2]:
        e.start()
    loop(9, lambda i: unit(m4(x + 3 + i // 3), yh, m4(z + 3 + i % 3)))
    for o in range(3):
        for e in near[o]:
            e.start()

    def gw(n, slot):
        k = pl.multiple_of(n * 256, 256)
        cols = pl.ds(pl.multiple_of(c * C, C), C)
        out = dot(H[:, :, :, :, pl.ds(k, 256)].reshape(1024, 256), T[:, :, cols].reshape(1024, C), ((0,), (0,)))
        out = out + dot(HO[:, :, :, :, pl.ds(k, 256)].reshape(1024, 256), GX[...].reshape(1024, C), ((0,), (0,)))
        stage[slot] = out.astype(BF)

    def gw_copy(n, slot):
        k = pl.multiple_of(n * 256, 256)
        return pltpu.make_async_copy(stage.at[slot], gw_out.at[pl.ds(k, 256)], s_out.at[slot])

    def gw_tiles(lo_, hi_):
        def body(n, carry):
            slot = n % 2

            @pl.when(n >= 2)
            def _():
                gw_copy(n, slot).wait()

            gw(n, slot)
            gw_copy(n, slot).start()
            return carry

        lax.fori_loop(lo_, hi_, body, 0)

    def add_relay(o):
        ax = ORDERS[o][0]
        a = me[ax]
        for e in far[o]:
            e.wait_recv()

        def body(i, carry):
            u, w_ = i // 4, i % 4
            ip = at_of(o, (m4(a + 1),), first[o])
            im = at_of(o, (m4(a - 1),), second[o])
            others = [k for k in range(3) if k != ax]
            ip, im = list(ip), list(im)
            ip[others[0]], ip[others[1]] = u, w_
            im[others[0]], im[others[1]] = u, w_
            RB[o][u, w_, lo] = (RB[o][u, w_, lo].astype(F32) + SB[tuple(ip)].astype(F32)).astype(BF)
            RB[o][u, w_, hi[o]] = (RB[o][u, w_, hi[o]].astype(F32) + SB[tuple(im)].astype(F32)).astype(BF)
            return carry

        lax.fori_loop(0, 16, body, 0)
        for e in relay[o]:
            e.start()

    for e in GXC, *HX:
        e.wait_recv()

    def sum_cross(a):
        for e in cex[a]:
            e.wait()
        CT[a + 1] = CT[a] + CR[a, 0] + CR[a, 1] + CR[a, 2]

    sum_cross(0)
    for e in cex[1]:
        e.start()
    add_relay(0)
    gw_tiles(0, 2)
    add_relay(1)
    gw_tiles(2, 4)
    add_relay(2)
    sum_cross(1)
    for e in cex[2]:
        e.start()
    gw_tiles(4, 9)

    def second_phase(o):
        for e in near[o] + relay[o]:
            e.wait_recv()
        ax, bx, _ = ORDERS[o]
        others = [k for k in range(3) if k != ax]

        def body(i, carry):
            idx = list(at_of(o, (me[ax],), whole[o]))
            idx[others[0]], idx[others[1]] = i // 4, i % 4
            idx = tuple(idx)
            SB[idx] = (SB[idx].astype(F32) + RA[o][0, i // 4, i % 4].astype(F32)
                       + RA[o][1, i // 4, i % 4].astype(F32)).astype(BF)
            return carry

        lax.fori_loop(0, 16, body, 0)
        out = [send(SB.at[at_of(o, (me[ax], m4(me[bx] + k)), whole[o])], RC[o].at[k - 1], s_rc, (o, k - 1), along(bx, k))
               for k in (2, 1, 3)]
        for e in out:
            e.start()
        return out

    ph2 = []
    for o in range(3):
        ph2.append(second_phase(o))
        gw_tiles(9 + o, 10 + o)

    def third_phase(o):
        for e in ph2[o]:
            e.wait_recv()
        ax, bx, cx = ORDERS[o]

        def body(i, carry):
            idx = at_of(o, (me[ax], me[bx], i), whole[o])
            SB[idx] = (SB[idx].astype(F32) + RC[o][0, i].astype(F32) + RC[o][1, i].astype(F32)
                       + RC[o][2, i].astype(F32)).astype(BF)
            return carry

        lax.fori_loop(0, 4, body, 0)
        out = [send(SB.at[at_of(o, (*[me[k] for k in (ax, bx)], m4(me[cx] + k)), whole[o])], RD.at[k - 1, whole[o]], s_rd,
                    (o, k - 1), along(cx, k)) for k in (2, 1, 3)]
        for e in out:
            e.start()
        return out

    ph3 = [third_phase(o) for o in range(3)]
    gw_tiles(12, 14)
    sum_cross(2)
    b_me = x * 2 + p
    kl_out[...] = (CT[3, pl.ds(b_me, 1), :] - LSE[1, pl.ds(b_me, 1), :]) + LSE[0, pl.ds(b_me, 1), :]
    for o in range(3):
        for e in ph3[o]:
            e.wait_recv()
    for g, r in ((0, 128), (1, 128), (2, 128), (3, 64)):
        rows = pl.ds(g * 128, r)
        total = SB[x, y, z, rows].astype(F32)
        for k in range(3):
            total = total + RD[k, rows].astype(F32)
        FIN[0, pl.ds(0, r)] = total
        gh_out[:, g * 128:g * 128 + r] = FIN[0].T[:, 0:r].astype(BF)

    for n in (12, 13):
        gw_copy(n, n % 2).wait()
    for e in X + Y0 + Y1 + A + [WC, GXC] + HX:
        e.wait_send()
    for i in range(3):
        for q in range(2):
            for r in range(2):
                Z[i][q][r].wait_send()
                FW[i][q][r].wait_send()
    for o in range(3):
        for e in far[o] + near[o] + relay[o] + ph2[o] + ph3[o]:
            e.wait_send()


def local(hidden, head_weight, teacher_logits, upstream):
    t2 = teacher_logits.reshape(128, 16 * C)
    any_ = pl.BlockSpec(memory_space=pl.ANY)
    vmem = pl.BlockSpec(memory_space=pltpu.VMEM)
    dma = pltpu.SemaphoreType.DMA
    scratch = [
        pltpu.VMEM((4, 2, 4, 32, D), BF),
        pltpu.VMEM((4, 2, 4, 32, D), BF),
        pltpu.VMEM((2, D, C), BF),
        pltpu.VMEM((8, 128, 2 * C), BF),
        pltpu.VMEM((4, 2, 4, 32, 2 * C), F32),
        pltpu.VMEM((8, 128, C), BF),
        pltpu.VMEM((4, 4, 4, F, 128), BF),
        *[pltpu.VMEM((2, 4, 4, n, 128), BF) for n in COUNT],
        *[pltpu.VMEM((4, 4, n, 128), BF) for n in COUNT],
        *[pltpu.VMEM((3, 4, n, 128), BF) for n in COUNT],
        pltpu.VMEM((3, F, 128), BF),
        pltpu.VMEM((4, 2, 4, 32, 128), F32),
        pltpu.VMEM((4, 2, 4, 32, 128), F32),
        pltpu.VMEM((4, 4, 8, 128), F32),
        pltpu.VMEM((3, 3, 4, 8, 128), F32),
        pltpu.VMEM((4, 8, 128), F32),
        pltpu.VMEM((3, 3, 8, 128), F32),
        pltpu.VMEM((2, 8, 128), F32),
        pltpu.VMEM((4, 128, 128), F32),
        pltpu.VMEM((2, 256, C), BF),
        dma((6,)), dma((2, 3)), dma((2, 4)), dma((2, 3)), dma((2, 3, 2, 2)), dma((2, 3, 2, 2)), dma((2, 7)), dma((2,)),
        dma((2, 4)), dma((2,)), dma((2, 3, 3)), dma((2, 3, 3)), dma((2, 3, 2)), dma((2, 3, 4)), dma((2, 3, 3)),
        dma((2, 3, 3)), dma((2,)),
    ]
    gh, gw, kl = pl.pallas_call(
        kernel,
        out_shape=[jax.ShapeDtypeStruct((128, F), BF), jax.ShapeDtypeStruct((D, C), BF),
                   jax.ShapeDtypeStruct((1, 128), F32)],
        in_specs=[any_, any_, any_, vmem],
        out_specs=[vmem, any_, vmem],
        scratch_shapes=scratch,
        compiler_params=pltpu.CompilerParams(collective_id=0, has_side_effects=True, vmem_limit_bytes=63 * 2**20),
        cost_estimate=pl.CostEstimate(flops=45 * 10**9, bytes_accessed=60 * 2**20, transcendentals=8 * 2**20),
    )(hidden, head_weight, t2, upstream.reshape(16, 128))
    return gh, gw, kl.reshape(128)


def solution(mesh):
    return jax.shard_map(
        local,
        mesh=mesh,
        in_specs=(P("dp", None), P(None, ("dp", "vocab")), P("dp", None, "vocab"), P()),
        out_specs=(P("dp", "vocab"), P(None, ("dp", "vocab")), P("dp")),
        check_vma=False,
    )
```

```python
import jax
import jax.numpy as jnp
from jax import lax
from jax.experimental import pallas as pl
from jax.experimental.pallas import tpu as pltpu
from jax.sharding import PartitionSpec as P

D = 3584
F = 448
C = 1024
BF = jnp.bfloat16
F32 = jnp.float32
MESH = pl.DeviceIdType.MESH
START = (0, 128, 288)
COUNT = (128, 160, 160)
HALF = (64, 80, 80)


def m4(a):
    return (a + 8) % 4


def dot(a, b, dims):
    return lax.dot_general(a, b, (dims, ((), ())), preferred_element_type=F32)


def loop(n, f):
    def body(i, carry):
        f(i)
        return carry

    lax.fori_loop(0, n, body, 0)


def kernel(hid, w, t_in, up, gh_out, gw_out, kl_out, H, HO, W2, T, S, GX, SB, RA0, RA1, RA2, RB0, RB1, RB2, RC0, RC1,
           RC2, RD, PM, PS, ST, SR, CT, CR, LSE, FIN, stage, s_loc, s_in, s_x, s_y0, s_y, s_yb, s_z, s_f, s_a, s_w, s_h, s_g,
           s_st, s_ct, s_r0, s_r1, s_c0, s_c1, s_c2, s_rd, s_out, s_free):
    d = lax.axis_index("dp")
    v = lax.axis_index("vocab")
    x = d // 4
    p = (d // 2) % 2
    c = d % 2
    yh = v // 4
    y = yh * 2 + p
    z = v % 4
    me = (x, y, z)

    def dev(xx, yy, zz, cc):
        return (xx * 4 + (yy % 2) * 2 + cc, (yy // 2) * 4 + zz)

    def along(axis, k):
        at = [x, y, z]
        at[axis] = m4(at[axis] + k)
        return dev(*at, c)

    sibling = dev(x, y, z, 1 - c)
    yn = m4(y - 1 + 2 * p)
    yl = y + 1 - 2 * p
    dyn = dev(x, yn, z, c)
    dyl = dev(x, yl, z, c)
    xt = [m4(x + 1), m4(x - 1), m4(x + 2)]
    xq = [m4(x - 1), m4(x + 1), m4(x + 2)]
    xk = [m4(x + 2), m4(x + 1), m4(x - 1), x]
    dz = [along(2, 1), along(2, -1)]
    zq = [m4(z - 1), m4(z + 1)]
    a2a = [(x, yl), (xt[2], y), (xt[0], yl), (xt[1], y), (xt[2], yl), (xt[0], y), (xt[1], yl)]
    da = [dev(a, b, z, c) for a, b in a2a]

    partners = [along(a, k) for a in range(3) for k in (1, 2, 3)] + [sibling, da[2], da[4], da[6]]
    barrier = pltpu.get_barrier_semaphore()
    for to in partners:
        pl.semaphore_signal(barrier, inc=1, device_id=to, device_id_type=MESH)
    pl.semaphore_wait(barrier, len(partners))

    def send(src, dst, sems, at, to):
        return pltpu.make_async_remote_copy(
            src_ref=src, dst_ref=dst, send_sem=sems.at[(0, *at)], recv_sem=sems.at[(1, *at)],
            device_id=to, device_id_type=MESH)

    own = pl.ds(pl.multiple_of(z * 32, 32), 32)
    cols_c = pl.ds(pl.multiple_of(c * C, C), C)
    X = [send(hid.at[own], H.at[x, p, z], s_x, (i,), along(0, (1, -1, 2)[i])) for i in range(3)]
    A = [send(HO.at[a, b % 2, :, :, 0:2 * C], T.at[x, p], s_a, (k,), da[k]) for k, (a, b) in enumerate(a2a)]
    Y0 = [send(hid.at[pl.ds(pl.multiple_of(m4(z + k) * 32, 32), 32)], H.at[x, p, m4(z + k)], s_y0, (k,), dyn)
          for k in range(4)]
    low, high = pl.ds(0, 16), pl.ds(16, 16)
    Y1 = [send(H.at[xq[i], p, z], H.at[xq[i], p, z], s_y, (i,), dyn) for i in range(2)]
    Y1.append(send(H.at[xq[2], p, z, high], H.at[xq[2], p, z, high], s_y, (2,), dyn))
    YB = [send(H.at[xq[2], p, zz, low], H.at[xq[2], p, zz, low], s_yb, (k,), dyn)
          for k, zz in enumerate((z, zq[0], zq[1], m4(z + 2)))]
    pairs = [(2, 0), (0, 0), (1, 0), (0, 1), (1, 1), (2, 1)]

    def piece(i, q, zz):
        at = H.at[xq[i], (p + q) % 2, zz]
        return at.at[high] if (i, q) == (2, 1) else at

    def part_of(i, q, zz, r):
        if (i, q) == (2, 1):
            return H.at[xq[i], (p + q) % 2, zz, high, r * (D // 2):(r + 1) * (D // 2)]
        return H.at[xq[i], (p + q) % 2, zz, pl.ds(16 * r, 16)]

    Z = {(i, q): [send(piece(i, q, z), piece(i, q, z), s_z, (i, q, r), dz[r]) for r in range(2)] for i, q in pairs}
    FW = {(i, q): [send(part_of(i, q, zq[r], r), part_of(i, q, zq[r], r), s_f, (i, q, r), dz[r]) for r in range(2)]
          for i, q in pairs}
    WC = send(w, W2.at[:, cols_c], s_w, (), sibling)
    local = [pltpu.make_async_copy(hid.at[pl.ds(32 * k, 32)], H.at[x, p, k], s_loc.at[k]) for k in range(4)]
    local.append(pltpu.make_async_copy(w, W2.at[:, cols_c], s_loc.at[4]))
    for e in X:
        e.start()
    Y0[0].start()

    def t_copy(n, slot):
        return pltpu.make_async_copy(
            t_in.at[pl.ds(pl.multiple_of(n * 256, 256), 256)], stage.at[slot, 0:256], s_in.at[slot])

    t_copy(0, 0).start()
    t_copy(1, 1).start()
    row = lax.broadcasted_iota(jnp.int32, (256, 256), 0)
    col = lax.broadcasted_iota(jnp.int32, (256, 256), 1)
    swap = jnp.where(((row >> 4) == (col & 15)) & ((row & 15) == (col >> 4)), 1.0, 0.0).astype(BF)
    for n in range(8):
        t_copy(n, n % 2).wait()
        moved = jnp.dot(swap, stage[n % 2, 0:256], preferred_element_type=F32).astype(BF)
        if n < 6:
            t_copy(n + 2, n % 2).start()
        for a in range(16):
            HO[a // 4, (a // 2) % 2, n // 2, pl.ds((n % 2) * 16, 16), pl.ds((a % 2) * C, C)] = moved[a * 16:a * 16 + 16]
    WC.start()
    for l in local:
        l.start()
    local.append(pltpu.make_async_copy(HO.at[x, p, :, :, 0:2 * C], T.at[x, p], s_loc.at[5]))
    local[5].start()
    for i in range(3):
        X[i].wait_recv()
        Y1[i].start()
        if i == 2:
            YB[0].start()
        for r in range(2):
            Z[i, 0][r].start()
    for e in A:
        e.start()
    for k in range(1, 4):
        Y0[k].start()

    def teacher(i):
        rows = pl.ds(pl.multiple_of(i * 32, 32), 32)

        def top_of(e, top):
            for g in range(16):
                top = jnp.maximum(top, HO[e // 2, e % 2, i, :, g * 128:(g + 1) * 128].astype(F32))
            return top

        top = lax.fori_loop(0, 8, top_of, jnp.full((32, 128), -1e30, F32))

        def total_of(e, total):
            for g in range(16):
                total = total + jnp.exp(HO[e // 2, e % 2, i, :, g * 128:(g + 1) * 128].astype(F32) - top)
            return total

        FIN[0, rows] = top
        FIN[1, rows] = lax.fori_loop(0, 8, total_of, jnp.zeros((32, 128), F32))

    def merge(top, total):
        top, total = top.T, total.T
        peak = jnp.max(top, axis=0, keepdims=True)
        return peak, jnp.sum(total * jnp.exp(top - peak), axis=0, keepdims=True)

    ST[0, 2] = jnp.full((8, 128), -1e30, F32)
    ST[0, 3] = jnp.zeros((8, 128), F32)
    for i in range(3):
        Y1[i].wait_recv()
        for r in range(2):
            Z[i, 1][r].start()
    loop(4, teacher)
    peak_t, total_t = merge(FIN[0], FIN[1])
    ST[0, 2, pl.ds(x * 2 + p, 1), :] = peak_t
    ST[0, 3, pl.ds(x * 2 + p, 1), :] = total_t
    for l in local[:5]:
        l.wait()
    Y0[0].wait_recv()
    YB[0].wait_recv()
    WC.wait_recv()

    def student(zz):
        def tile(n):
            k = pl.ds(pl.multiple_of(n * C, C), C)
            out = jnp.dot(H[:, :, zz].reshape(256, D), W2[:, k], preferred_element_type=F32)
            S[:, :, zz, :, k] = out.reshape(4, 2, 32, C)

        loop(2, tile)

        def stats(b, carry):
            xx, pp = b // 2, b % 2
            top = S[xx, pp, zz, :, 0:128]
            for g in range(1, 16):
                top = jnp.maximum(top, S[xx, pp, zz, :, g * 128:(g + 1) * 128])
            total = jnp.zeros((32, 128), F32)
            for g in range(16):
                total = total + jnp.exp(S[xx, pp, zz, :, g * 128:(g + 1) * 128] - top)
            PM[xx, pp, zz] = top
            PS[xx, pp, zz] = total
            return carry

        lax.fori_loop(0, 8, stats, 0)

    student(z)
    for i, q in pairs:
        for r in range(2):
            Z[i, q][r].wait_recv()
            if (i, q) == (2, 0):
                YB[1 + r].start()
            FW[i, q][r].start()
        if (i, q) == (1, 0):
            for r in range(2):
                FW[2, 0][r].wait_recv()
            YB[3].start()
    for k in range(1, 4):
        Y0[k].wait_recv()
    for r in range(2):
        YB[1 + r].wait_recv()
        student(zq[r])
    for i, q in pairs[1:]:
        for r in range(2):
            FW[i, q][r].wait_recv()
    YB[3].wait_recv()
    student(m4(z + 2))

    def merge_student(b, carry):
        xx, pp = b // 2, b % 2
        peak, total = merge(PM[xx, pp].reshape(128, 128), PS[xx, pp].reshape(128, 128))
        ST[0, 0, pl.ds(b, 1), :] = peak
        ST[0, 1, pl.ds(b, 1), :] = total
        return carry

    lax.fori_loop(0, 8, merge_student, 0)

    for a in range(3):
        ex = [send(ST.at[a], SR.at[a, k], s_st, (a, k), along(a, k + 1)) for k in range(3)]
        for e in ex:
            e.start()
        for e in (X + Y0 + Y1 + YB + [WC], [e for at in pairs[:3] for e in Z[at] + FW[at]],
                  [e for at in pairs[3:] for e in Z[at] + FW[at]])[a]:
            e.wait_send()
        for e in ex:
            e.wait()
        for s in range(2):
            tops = [ST[a, 2 * s]] + [SR[a, k, 2 * s] for k in range(3)]
            sums = [ST[a, 2 * s + 1]] + [SR[a, k, 2 * s + 1] for k in range(3)]
            peak = jnp.maximum(jnp.maximum(tops[0], tops[1]), jnp.maximum(tops[2], tops[3]))
            total = sum(u * jnp.exp(t - peak) for t, u in zip(tops, sums))
            ST[a + 1, 2 * s] = peak
            ST[a + 1, 2 * s + 1] = total
    LSE[0] = ST[3, 0] + jnp.log(ST[3, 1])
    LSE[1] = ST[3, 2] + jnp.log(ST[3, 3])

    def grads(b):
        def spread(row):
            return jnp.broadcast_to(row, (128, 128)).T

        FIN[0] = spread(LSE[0, pl.ds(b, 1), :])
        FIN[1] = spread(LSE[1, pl.ds(b, 1), :])
        FIN[2] = spread(up[pl.ds(2 * b + c, 1), :])
        xx, pp = b // 2, b % 2

        def part(i):
            rows = pl.ds(pl.multiple_of(i * 32, 32), 32)
            ls, lt, u = FIN[0, rows], FIN[1, rows], FIN[2, rows]
            cross = jnp.zeros((32, 128), F32)
            for g in range(16):
                at = slice(g * 128, (g + 1) * 128)
                s = S[xx, pp, i, :, at]
                t = T[xx, pp, i, :, at].astype(F32)
                pt = jnp.exp(t - lt)
                cross = cross + pt * (t - s)
                T[xx, pp, i, :, at] = (u * (jnp.exp(s - ls) - pt)).astype(BF)
            FIN[3, rows] = cross

        loop(4, part)
        CT[0, pl.ds(b, 1), :] = jnp.sum(FIN[3].T, axis=0, keepdims=True)

    def units(xx):
        def half(n):
            hh = (1 - yh + n // 2) % 2
            feat = pl.ds(pl.multiple_of((hh * 4 + n % 2 * 2) * F, 2 * F), 2 * F)
            out = dot(W2[feat, :], T[xx].reshape(256, 2 * C), ((1,), (1,))).astype(BF)
            for i in range(2):
                SB[xx, 2 * hh, n % 2 * 2 + i] = out[i * F:(i + 1) * F, 0:128]
                SB[xx, 2 * hh + 1, n % 2 * 2 + i] = out[i * F:(i + 1) * F, 128:256]

        loop(4, half)

    RA, RB = (RA0, RA1, RA2), (RB0, RB1, RB2)
    first = [pl.ds(START[o], HALF[o]) for o in range(3)]
    second = [pl.ds(START[o] + HALF[o], COUNT[o] - HALF[o]) for o in range(3)]
    whole = [pl.ds(START[o], COUNT[o]) for o in range(3)]
    lo = [pl.ds(0, HALF[o]) for o in range(3)]
    hi = [pl.ds(HALF[o], COUNT[o] - HALF[o]) for o in range(3)]

    def plus_into(dst, i, *terms):
        total = dst[i].astype(F32)
        for ref, j in terms:
            total = total + ref[j].astype(F32)
        dst[i] = total.astype(BF)

    far0 = [send(SB.at[xk[0], :, :, first[0]], RB0.at[:, :, lo[0]], s_r0, (0,), along(0, 1)),
            send(SB.at[xk[0], :, :, second[0]], RB0.at[:, :, hi[0]], s_r0, (1,), along(0, -1))]
    near0 = [send(SB.at[xk[1], :, :, second[0]], RA0.at[0, :, :, hi[0]], s_r0, (2,), along(0, 1)),
             send(SB.at[xk[2], :, :, first[0]], RA0.at[1, :, :, lo[0]], s_r0, (3,), along(0, -1))]
    relay0 = [send(RB0.at[:, :, lo[0]], RA0.at[0, :, :, lo[0]], s_r0, (4,), along(0, 1)),
              send(RB0.at[:, :, hi[0]], RA0.at[1, :, :, hi[0]], s_r0, (5,), along(0, -1))]
    P2_0 = [send(SB.at[x, m4(y + j), :, whole[0]], RC0.at[j - 1], s_c0, (j - 1,), along(1, j)) for j in (2, 1, 3)]
    P3_0 = [send(SB.at[x, y, m4(z + j), whole[0]], RD.at[j - 1, whole[0]], s_rd, (0, j - 1), along(2, j)) for j in (2, 1, 3)]

    def sl(o, xx, a, u, rows):
        return (xx, a, u, rows) if o == 1 else (xx, u, a, rows)

    full = slice(None)

    def hop(o, k):
        a, xx = me[o], xk[k]
        plus, minus = along(o, 1), along(o, -1)
        n = (o - 1, k)
        return [
            send(SB.at[sl(o, xx, m4(a + 2), full, first[o])], RB[o].at[xx, :, lo[o]], s_r1, (*n, 0), plus),
            send(SB.at[sl(o, xx, m4(a + 2), full, second[o])], RB[o].at[xx, :, hi[o]], s_r1, (*n, 1), minus),
            send(SB.at[sl(o, xx, m4(a + 1), full, second[o])], RA[o].at[0, xx, :, hi[o]], s_r1, (*n, 2), plus),
            send(SB.at[sl(o, xx, m4(a - 1), full, first[o])], RA[o].at[1, xx, :, lo[o]], s_r1, (*n, 3), minus),
            send(RB[o].at[xx, :, lo[o]], RA[o].at[0, xx, :, lo[o]], s_r1, (*n, 4), plus),
            send(RB[o].at[xx, :, hi[o]], RA[o].at[1, xx, :, hi[o]], s_r1, (*n, 5), minus)]

    hops = {(o, k): hop(o, k) for o in (1, 2) for k in range(4)}
    P2_1 = [[send(SB.at[xk[k], y, m4(z + j), whole[1]], RC1.at[j - 1, xk[k]], s_c1, (k, j - 1), along(2, j))
             for j in (2, 1, 3)] for k in range(4)]
    rel = (2, 1, 3)
    P3_1 = [send(SB.at[xk[k], y, z, whole[1]], RD.at[rel[k] - 1, whole[1]], s_rd, (1, rel[k] - 1), along(0, rel[k]))
            for k in range(3)]
    P2_2 = [send(SB.at[xk[k], :, z, whole[2]], RC2.at[rel[k] - 1], s_c2, (rel[k] - 1,), along(0, rel[k])) for k in range(3)]
    P3_2 = [send(SB.at[x, m4(y + j), z, whole[2]], RD.at[j - 1, whole[2]], s_rd, (2, j - 1), along(1, j)) for j in (2, 1, 3)]

    def start_hops(k):
        for n in range(4):
            for o in (1, 2):
                hops[o, k][n].start()

    def relay_hops(k):
        xx = xk[k]
        for o in (1, 2):
            for e in hops[o, k][:2]:
                e.wait_recv()

            def add(u, o=o):
                a = me[o]
                plus_into(RB[o], (xx, u, lo[o]), (SB, sl(o, xx, m4(a + 1), u, first[o])))
                plus_into(RB[o], (xx, u, hi[o]), (SB, sl(o, xx, m4(a - 1), u, second[o])))

            loop(4, add)
            for e in hops[o, k][4:]:
                e.start()

    def finish_hops(k):
        xx = xk[k]
        for o in (1, 2):
            for e in hops[o, k][2:]:
                e.wait_recv()

            def add(u, o=o):
                plus_into(SB, sl(o, xx, me[o], u, whole[o]), (RA[o], (0, xx, u)), (RA[o], (1, xx, u)))

            loop(4, add)
            for e in (P2_1[k] if o == 1 else P2_2[k:k + 1]):
                e.start()

    def finish_1(k):
        for e in P2_1[k]:
            e.wait_recv()
        plus_into(SB, (xk[k], y, z, whole[1]), *[(RC1, (j, xk[k])) for j in range(3)])
        if k < 3:
            P3_1[k].start()

    def relay_0(r):
        far0[r].wait_recv()
        rows, mine = ((lo, first), (hi, second))[r]

        def add(i):
            plus_into(RB0, (i // 4, i % 4, rows[0]), (SB, (xk[1 + r], i // 4, i % 4, mine[0])))

        loop(16, add)
        relay0[r].start()

    def gw_copy(n):
        m = (n + 4) % 7
        return pltpu.make_async_copy(stage.at[n % 2], gw_out.at[pl.ds(m * 512, 512)], s_out.at[n % 2])

    def gw(n):
        k = pl.ds((n + 4) % 7 * 512, 512)
        if n > 1:
            gw_copy(n - 2).wait()
        out = dot(H[:, :, :, :, k].reshape(1024, 512), T[:, :, :, :, cols_c].reshape(1024, C), ((0,), (0,)))
        out = out + dot(HO[:, :, :, :, k].reshape(1024, 512), GX[...].reshape(1024, C), ((0,), (0,)))
        stage[n % 2] = out.astype(BF)
        gw_copy(n).start()

    HXA = [send(H.at[xx, :, :, :, 2 * C:D], HO.at[xx, :, :, :, 2 * C:D], s_h, (0, xx), sibling) for xx in range(4)]
    HXB = [send(H.at[xx, :, :, :, 0:2 * C], HO.at[xx, :, :, :, 0:2 * C], s_h, (1, xx), sibling) for xx in range(4)]
    GXC = [send(T.at[xx, :, :, :, pl.ds(pl.multiple_of((1 - c) * C, C), C)], GX.at[xx], s_g, (k,), sibling)
           for k, xx in enumerate(xk)]
    cex = [[send(CT.at[a], CR.at[a, k], s_ct, (a, k), along(a, k + 1)) for k in range(3)] for a in range(3)]

    def sum_cross(a):
        for e in cex[a]:
            e.wait()
        CT[a + 1] = CT[a] + CR[a, 0] + CR[a, 1] + CR[a, 2]
        if a < 2:
            for e in cex[a + 1]:
                e.start()

    for k in range(4):
        for n in ((1, 4), (3, 6), (5, 2), (0,))[k]:
            A[n].wait_recv()
        if k == 3:
            local[5].wait()
        for q in range(2):
            grads(2 * xk[k] + q)
        units(xk[k])
        start_hops(k)
        if k == 0:
            for e in far0:
                e.start()
        if k in (1, 2):
            near0[k - 1].start()
        GXC[k].start()
        if k == 1:
            for e in HXA:
                e.start()
        if k == 3:
            for e in A:
                e.wait_send()
            pl.semaphore_signal(s_free, inc=1, device_id=sibling, device_id_type=MESH)
        if k > 0:
            relay_hops(k - 1)
        if k in (1, 2):
            relay_0(k - 1)
        if k > 1:
            finish_hops(k - 2)
    for e in cex[0]:
        e.start()
    finish_1(0)
    pl.semaphore_wait(s_free, 1)
    for e in HXB:
        e.start()
    for e in GXC + HXA:
        e.wait_recv()
    gw(0)
    relay_hops(3)
    finish_hops(2)
    for e in near0 + relay0:
        e.wait_recv()

    def add_0(i):
        plus_into(SB, (x, i // 4, i % 4, whole[0]), (RA0, (0, i // 4, i % 4)), (RA0, (1, i // 4, i % 4)))

    loop(16, add_0)
    for e in P2_0:
        e.start()
    finish_1(1)
    sum_cross(0)
    gw(1)
    finish_hops(3)
    finish_1(2)
    sum_cross(1)
    gw(2)
    for e in P2_0 + P2_2:
        e.wait_recv()

    def add_1(u):
        plus_into(SB, (x, y, u, whole[0]), *[(RC0, (j, u)) for j in range(3)])
        plus_into(SB, (x, u, z, whole[2]), *[(RC2, (j, u)) for j in range(3)])

    loop(4, add_1)
    for e in P3_0 + P3_2:
        e.start()
    for e in HXB:
        e.wait_recv()
    gw(3)
    finish_1(3)
    sum_cross(2)
    gw(4)
    gw(5)
    gw(6)
    b_me = x * 2 + p
    kl_out[...] = (CT[3, pl.ds(b_me, 1), :] - LSE[1, pl.ds(b_me, 1), :]) + LSE[0, pl.ds(b_me, 1), :]
    for e in P3_0 + P3_1 + P3_2:
        e.wait_recv()
    total = SB[x, y, z].astype(F32)
    for k in range(3):
        total = total + RD[k].astype(F32)
    gh_out[...] = total.astype(BF)

    for n in (5, 6):
        gw_copy(n).wait()
    for e in GXC + HXA + HXB:
        e.wait_send()
    for e in far0 + near0 + relay0 + P2_0 + P3_0 + P3_1 + P2_2 + P3_2:
        e.wait_send()
    for k in range(4):
        for e in hops[1, k] + hops[2, k] + P2_1[k]:
            e.wait_send()


def write_out(src, dst, held, sems):
    rows = [pl.ds(n * (D // 14), D // 14) for n in range(14)]
    into = [pltpu.make_async_copy(src.at[r], held.at[r], sems.at[0, n]) for n, r in enumerate(rows)]
    out = [pltpu.make_async_copy(held.at[r], dst.at[r], sems.at[1, n]) for n, r in enumerate(rows)]
    for e in into:
        e.start()
    for a, b in zip(into, out):
        a.wait()
        b.start()
    for e in out:
        e.wait()


def local(hidden, head_weight, teacher_logits, upstream):
    any_ = pl.BlockSpec(memory_space=pl.ANY)
    vmem = pl.BlockSpec(memory_space=pltpu.VMEM)
    dma = pltpu.SemaphoreType.DMA
    scratch = [
        pltpu.VMEM((4, 2, 4, 32, D), BF),
        pltpu.VMEM((4, 2, 4, 32, D), BF),
        pltpu.VMEM((D, 2 * C), BF),
        pltpu.VMEM((4, 2, 4, 32, 2 * C), BF),
        pltpu.VMEM((4, 2, 4, 32, 2 * C), F32),
        pltpu.VMEM((4, 2, 4, 32, C), BF),
        pltpu.VMEM((4, 4, 4, F, 128), BF),
        *[pltpu.VMEM((2, 4, 4, n, 128), BF) for n in COUNT],
        *[pltpu.VMEM((4, 4, n, 128), BF) for n in COUNT],
        *[pltpu.VMEM((3, 4, n, 128), BF) for n in COUNT],
        pltpu.VMEM((3, F, 128), BF),
        pltpu.VMEM((4, 2, 4, 32, 128), F32),
        pltpu.VMEM((4, 2, 4, 32, 128), F32),
        pltpu.VMEM((4, 4, 8, 128), F32),
        pltpu.VMEM((3, 3, 4, 8, 128), F32),
        pltpu.VMEM((4, 8, 128), F32),
        pltpu.VMEM((3, 3, 8, 128), F32),
        pltpu.VMEM((2, 8, 128), F32),
        pltpu.VMEM((4, 128, 128), F32),
        pltpu.VMEM((2, 512, C), BF),
        dma((6,)), dma((2,)), dma((2, 3)), dma((2, 4)), dma((2, 3)), dma((2, 4)), dma((2, 3, 2, 2)), dma((2, 3, 2, 2)),
        dma((2, 7)), dma((2,)), dma((2, 2, 4)), dma((2, 4)), dma((2, 3, 3)), dma((2, 3, 3)), dma((2, 6)), dma((2, 2, 4, 6)),
        dma((2, 3)), dma((2, 4, 3)), dma((2, 3)), dma((2, 3, 3)), dma((2,)), pltpu.SemaphoreType.REGULAR,
    ]
    gh, gw, kl = pl.pallas_call(
        kernel,
        out_shape=[jax.ShapeDtypeStruct((F, 128), BF), jax.ShapeDtypeStruct((D, C), BF),
                   jax.ShapeDtypeStruct((1, 128), F32)],
        in_specs=[any_, any_, any_, vmem],
        out_specs=[vmem, any_, vmem],
        scratch_shapes=scratch,
        compiler_params=pltpu.CompilerParams(collective_id=0, has_side_effects=True, vmem_limit_bytes=64 * 2**20 - 65536),
        cost_estimate=pl.CostEstimate(flops=45 * 10**9, bytes_accessed=60 * 2**20, transcendentals=8 * 2**20),
    )(hidden, head_weight, teacher_logits.reshape(2 * C, C), upstream.reshape(16, 128))
    gw = pl.pallas_call(
        write_out,
        out_shape=jax.ShapeDtypeStruct((D, C), BF),
        in_specs=[any_],
        out_specs=any_,
        scratch_shapes=[pltpu.VMEM((D, C), BF), dma((2, 14))],
        compiler_params=pltpu.CompilerParams(vmem_limit_bytes=60 * 2**20),
        cost_estimate=pl.CostEstimate(flops=0, bytes_accessed=14 * 2**20, transcendentals=0),
    )(gw)
    return gh.T, gw, kl.reshape(128)


def solution(mesh):
    return jax.shard_map(
        local,
        mesh=mesh,
        in_specs=(P("dp", None), P(None, ("dp", "vocab")), P("dp", None, "vocab"), P()),
        out_specs=(P("dp", "vocab"), P(None, ("dp", "vocab")), P("dp")),
        check_vma=False,
    )
```

```python
import jax
import jax.numpy as jnp
from jax import lax
from jax.experimental import pallas as pl
from jax.experimental.pallas import tpu as pltpu
from jax.sharding import PartitionSpec as P

D = 3584
F = 448
C = 1024
BF = jnp.bfloat16
F32 = jnp.float32
MESH = pl.DeviceIdType.MESH
START = (0, 128, 288)
COUNT = (128, 160, 160)
HALF = (64, 80, 80)


def m4(a):
    return (a + 8) % 4


def dot(a, b, dims):
    return lax.dot_general(a, b, (dims, ((), ())), preferred_element_type=F32)


def loop(n, f):
    def body(i, carry):
        f(i)
        return carry

    lax.fori_loop(0, n, body, 0)


def kernel(hid, w, t_in, up, gh_out, gw_out, kl_out, H, HO, W2, T, S, GX, SB, RA0, RA1, RA2, RB0, RB1, RB2, RC0, RC1,
           RC2, RD, PM, PS, ST, SR, CT, CR, LSE, FIN, stage, s_loc, s_in, s_x, s_y0, s_y, s_yb, s_z, s_f, s_a, s_w, s_h, s_g,
           s_st, s_ct, s_r0, s_r1, s_c0, s_c1, s_c2, s_rd, s_out, s_free):
    d = lax.axis_index("dp")
    v = lax.axis_index("vocab")
    x = d // 4
    p = (d // 2) % 2
    c = d % 2
    yh = v // 4
    y = yh * 2 + p
    z = v % 4
    me = (x, y, z)

    def dev(xx, yy, zz, cc):
        return (xx * 4 + (yy % 2) * 2 + cc, (yy // 2) * 4 + zz)

    def along(axis, k):
        at = [x, y, z]
        at[axis] = m4(at[axis] + k)
        return dev(*at, c)

    sibling = dev(x, y, z, 1 - c)
    yn = m4(y - 1 + 2 * p)
    yl = y + 1 - 2 * p
    dyn = dev(x, yn, z, c)
    dyl = dev(x, yl, z, c)
    xt = [m4(x + 1), m4(x - 1), m4(x + 2)]
    xq = [m4(x - 1), m4(x + 1), m4(x + 2)]
    xk = [m4(x + 2), m4(x + 1), m4(x - 1), x]
    dz = [along(2, 1), along(2, -1)]
    zq = [m4(z - 1), m4(z + 1)]
    a2a = [(x, yl), (xt[2], y), (xt[0], yl), (xt[1], y), (xt[2], yl), (xt[0], y), (xt[1], yl)]
    da = [dev(a, b, z, c) for a, b in a2a]

    partners = [along(a, k) for a in range(3) for k in (1, 2, 3)] + [sibling, da[2], da[4], da[6]]
    barrier = pltpu.get_barrier_semaphore()
    for to in partners:
        pl.semaphore_signal(barrier, inc=1, device_id=to, device_id_type=MESH)
    pl.semaphore_wait(barrier, len(partners))

    def send(src, dst, sems, at, to):
        return pltpu.make_async_remote_copy(
            src_ref=src, dst_ref=dst, send_sem=sems.at[(0, *at)], recv_sem=sems.at[(1, *at)],
            device_id=to, device_id_type=MESH)

    own = pl.ds(pl.multiple_of(z * 32, 32), 32)
    cols_c = pl.ds(pl.multiple_of(c * C, C), C)
    X = [send(hid.at[own], H.at[x, p, z], s_x, (i,), along(0, (1, -1, 2)[i])) for i in range(3)]
    A = [send(HO.at[a, b % 2, :, :, 0:2 * C], T.at[x, p], s_a, (k,), da[k]) for k, (a, b) in enumerate(a2a)]
    Y0 = [send(hid.at[pl.ds(pl.multiple_of(m4(z + k) * 32, 32), 32)], H.at[x, p, m4(z + k)], s_y0, (k,), dyn if k % 2 == 0 else dyl)
          for k in range(4)]
    Y1 = [send(H.at[xq[i], p, z], H.at[xq[i], p, z], s_y, (i,), dyn) for i in range(2)]
    YB = [send(H.at[xq[2], p, zz], H.at[xq[2], p, zz], s_yb, (k,), dyn)
          for k, zz in enumerate((z, zq[0], zq[1], m4(z + 2)))]
    pairs = [(2, 0), (0, 0), (1, 0), (0, 1), (1, 1)]

    def piece(i, q, zz):
        return H.at[xq[i], (p + q) % 2, zz]

    def part_of(i, q, zz, r):
        return H.at[xq[i], (p + q) % 2, zz, pl.ds(16 * r, 16)]

    Z = {(i, q): [send(piece(i, q, z), piece(i, q, z), s_z, (i, q, r), dz[r]) for r in range(2)] for i, q in pairs}
    FW = {(i, q): [send(part_of(i, q, zq[r], r), part_of(i, q, zq[r], r), s_f, (i, q, r), dz[r]) for r in range(2)]
          for i, q in pairs}
    WC = send(w, W2.at[:, cols_c], s_w, (), sibling)
    local = [pltpu.make_async_copy(hid.at[pl.ds(32 * k, 32)], H.at[x, p, k], s_loc.at[k]) for k in range(4)]
    local.append(pltpu.make_async_copy(w, W2.at[:, cols_c], s_loc.at[4]))
    for e in X:
        e.start()
    Y0[0].start()
    Y0[1].start()
    Y0[3].start()
    WC.start()
    for l in local:
        l.start()

    def t_copy(n, slot):
        return pltpu.make_async_copy(
            t_in.at[pl.ds(pl.multiple_of(n * 256, 256), 256)], stage.at[slot, 0:256], s_in.at[slot])

    t_copy(0, 0).start()
    t_copy(1, 1).start()
    row = lax.broadcasted_iota(jnp.int32, (256, 256), 0)
    col = lax.broadcasted_iota(jnp.int32, (256, 256), 1)
    swap = jnp.where(((row >> 4) == (col & 15)) & ((row & 15) == (col >> 4)), 1.0, 0.0).astype(BF)
    for n in range(8):
        t_copy(n, n % 2).wait()
        moved = jnp.dot(swap, stage[n % 2, 0:256], preferred_element_type=F32).astype(BF)
        if n < 6:
            t_copy(n + 2, n % 2).start()
        for a in range(16):
            HO[a // 4, (a // 2) % 2, n // 2, pl.ds((n % 2) * 16, 16), pl.ds((a % 2) * C, C)] = moved[a * 16:a * 16 + 16]
    local.append(pltpu.make_async_copy(HO.at[x, p, :, :, 0:2 * C], T.at[x, p], s_loc.at[5]))
    local[5].start()
    for i in range(3):
        X[i].wait_recv()
        (Y1 + YB)[i].start()
        for r in range(2):
            Z[i, 0][r].start()
    for e in A:
        e.start()
    Y0[2].start()

    def teacher(i):
        rows = pl.ds(pl.multiple_of(i * 32, 32), 32)

        def top_of(e, top):
            for g in range(16):
                top = jnp.maximum(top, HO[e // 2, e % 2, i, :, g * 128:(g + 1) * 128].astype(F32))
            return top

        top = lax.fori_loop(0, 8, top_of, jnp.full((32, 128), -1e30, F32))

        def total_of(e, total):
            for g in range(16):
                total = total + jnp.exp(HO[e // 2, e % 2, i, :, g * 128:(g + 1) * 128].astype(F32) - top)
            return total

        FIN[0, rows] = top
        FIN[1, rows] = lax.fori_loop(0, 8, total_of, jnp.zeros((32, 128), F32))

    def merge(top, total):
        top, total = top.T, total.T
        peak = jnp.max(top, axis=0, keepdims=True)
        return peak, jnp.sum(total * jnp.exp(top - peak), axis=0, keepdims=True)

    ST[0, 2] = jnp.full((8, 128), -1e30, F32)
    ST[0, 3] = jnp.zeros((8, 128), F32)
    for i in range(2):
        Y1[i].wait_recv()
        for r in range(2):
            Z[i, 1][r].start()
    loop(4, teacher)
    peak_t, total_t = merge(FIN[0], FIN[1])
    ST[0, 2, pl.ds(x * 2 + p, 1), :] = peak_t
    ST[0, 3, pl.ds(x * 2 + p, 1), :] = total_t
    for l in local[:5]:
        l.wait()
    Y0[0].wait_recv()
    YB[0].wait_recv()
    WC.wait_recv()

    def student(zz):
        def tile(n):
            k = pl.ds(pl.multiple_of(n * C, C), C)
            out = jnp.dot(H[:, :, zz].reshape(256, D), W2[:, k], preferred_element_type=F32)
            S[:, :, zz, :, k] = out.reshape(4, 2, 32, C)

        loop(2, tile)

        def stats(b, carry):
            xx, pp = b // 2, b % 2
            top = S[xx, pp, zz, :, 0:128]
            for g in range(1, 16):
                top = jnp.maximum(top, S[xx, pp, zz, :, g * 128:(g + 1) * 128])
            total = jnp.zeros((32, 128), F32)
            for g in range(16):
                total = total + jnp.exp(S[xx, pp, zz, :, g * 128:(g + 1) * 128] - top)
            PM[xx, pp, zz] = top
            PS[xx, pp, zz] = total
            return carry

        lax.fori_loop(0, 8, stats, 0)

    student(z)
    for i, q in pairs[:4]:
        for r in range(2):
            Z[i, q][r].wait_recv()
            if i == 2:
                YB[1 + r].start()
    for at in pairs[:3]:
        for r in range(2):
            FW[at][r].start()
    for r in range(2):
        Z[1, 1][r].wait_recv()
    for at in pairs[3:]:
        for r in range(2):
            FW[at][r].start()
    for k in range(1, 4):
        Y0[k].wait_recv()
    for r in range(2):
        YB[1 + r].wait_recv()
        student(zq[r])
        if r == 0:
            for n in range(2):
                FW[2, 0][n].wait_recv()
            YB[3].start()
    for i, q in pairs[1:]:
        for r in range(2):
            FW[i, q][r].wait_recv()
    YB[3].wait_recv()
    student(m4(z + 2))

    def merge_student(b, carry):
        xx, pp = b // 2, b % 2
        peak, total = merge(PM[xx, pp].reshape(128, 128), PS[xx, pp].reshape(128, 128))
        ST[0, 0, pl.ds(b, 1), :] = peak
        ST[0, 1, pl.ds(b, 1), :] = total
        return carry

    lax.fori_loop(0, 8, merge_student, 0)

    for a in range(3):
        ex = [send(ST.at[a], SR.at[a, k], s_st, (a, k), along(a, k + 1)) for k in range(3)]
        for e in ex:
            e.start()
        for e in (X + Y0 + Y1 + YB + [WC], [e for at in pairs[:3] for e in Z[at] + FW[at]],
                  [e for at in pairs[3:] for e in Z[at] + FW[at]])[a]:
            e.wait_send()
        for e in ex:
            e.wait()
        for s in range(2):
            tops = [ST[a, 2 * s]] + [SR[a, k, 2 * s] for k in range(3)]
            sums = [ST[a, 2 * s + 1]] + [SR[a, k, 2 * s + 1] for k in range(3)]
            peak = jnp.maximum(jnp.maximum(tops[0], tops[1]), jnp.maximum(tops[2], tops[3]))
            total = sum(u * jnp.exp(t - peak) for t, u in zip(tops, sums))
            ST[a + 1, 2 * s] = peak
            ST[a + 1, 2 * s + 1] = total
    LSE[0] = ST[3, 0] + jnp.log(ST[3, 1])
    LSE[1] = ST[3, 2] + jnp.log(ST[3, 3])

    def grads(b):
        def spread(row):
            return jnp.broadcast_to(row, (128, 128)).T

        FIN[0] = spread(LSE[0, pl.ds(b, 1), :])
        FIN[1] = spread(LSE[1, pl.ds(b, 1), :])
        FIN[2] = spread(up[pl.ds(2 * b + c, 1), :])
        xx, pp = b // 2, b % 2

        def part(i):
            rows = pl.ds(pl.multiple_of(i * 32, 32), 32)
            ls, lt, u = FIN[0, rows], FIN[1, rows], FIN[2, rows]
            cross = jnp.zeros((32, 128), F32)
            for g in range(16):
                at = slice(g * 128, (g + 1) * 128)
                s = S[xx, pp, i, :, at]
                t = T[xx, pp, i, :, at].astype(F32)
                pt = jnp.exp(t - lt)
                cross = cross + pt * (t - s)
                T[xx, pp, i, :, at] = (u * (jnp.exp(s - ls) - pt)).astype(BF)
            FIN[3, rows] = cross

        loop(4, part)
        CT[0, pl.ds(b, 1), :] = jnp.sum(FIN[3].T, axis=0, keepdims=True)

    def units(xx):
        def half(n):
            hh = (1 - yh + n // 2) % 2
            feat = pl.ds(pl.multiple_of((hh * 4 + n % 2 * 2) * F, 2 * F), 2 * F)
            out = dot(W2[feat, :], T[xx].reshape(256, 2 * C), ((1,), (1,))).astype(BF)
            for i in range(2):
                SB[xx, 2 * hh, n % 2 * 2 + i] = out[i * F:(i + 1) * F, 0:128]
                SB[xx, 2 * hh + 1, n % 2 * 2 + i] = out[i * F:(i + 1) * F, 128:256]

        loop(4, half)

    RA, RB = (RA0, RA1, RA2), (RB0, RB1, RB2)
    first = [pl.ds(START[o], HALF[o]) for o in range(3)]
    second = [pl.ds(START[o] + HALF[o], COUNT[o] - HALF[o]) for o in range(3)]
    whole = [pl.ds(START[o], COUNT[o]) for o in range(3)]
    lo = [pl.ds(0, HALF[o]) for o in range(3)]
    hi = [pl.ds(HALF[o], COUNT[o] - HALF[o]) for o in range(3)]

    def plus_into(dst, i, *terms):
        total = dst[i].astype(F32)
        for ref, j in terms:
            total = total + ref[j].astype(F32)
        dst[i] = total.astype(BF)

    far0 = [send(SB.at[xk[0], :, :, first[0]], RB0.at[:, :, lo[0]], s_r0, (0,), along(0, 1)),
            send(SB.at[xk[0], :, :, second[0]], RB0.at[:, :, hi[0]], s_r0, (1,), along(0, -1))]
    near0 = [send(SB.at[xk[1], :, :, second[0]], RA0.at[0, :, :, hi[0]], s_r0, (2,), along(0, 1)),
             send(SB.at[xk[2], :, :, first[0]], RA0.at[1, :, :, lo[0]], s_r0, (3,), along(0, -1))]
    relay0 = [send(RB0.at[:, :, lo[0]], RA0.at[0, :, :, lo[0]], s_r0, (4,), along(0, 1)),
              send(RB0.at[:, :, hi[0]], RA0.at[1, :, :, hi[0]], s_r0, (5,), along(0, -1))]
    P2_0 = [send(SB.at[x, m4(y + j), :, whole[0]], RC0.at[j - 1], s_c0, (j - 1,), along(1, j)) for j in (2, 1, 3)]
    P3_0 = [send(SB.at[x, y, m4(z + j), whole[0]], RD.at[j - 1, whole[0]], s_rd, (0, j - 1), along(2, j)) for j in (2, 1, 3)]

    def sl(o, xx, a, u, rows):
        return (xx, a, u, rows) if o == 1 else (xx, u, a, rows)

    full = slice(None)

    def hop(o, k):
        a, xx = me[o], xk[k]
        plus, minus = along(o, 1), along(o, -1)
        n = (o - 1, k)
        return [
            send(SB.at[sl(o, xx, m4(a + 2), full, first[o])], RB[o].at[xx, :, lo[o]], s_r1, (*n, 0), plus),
            send(SB.at[sl(o, xx, m4(a + 2), full, second[o])], RB[o].at[xx, :, hi[o]], s_r1, (*n, 1), minus),
            send(SB.at[sl(o, xx, m4(a + 1), full, second[o])], RA[o].at[0, xx, :, hi[o]], s_r1, (*n, 2), plus),
            send(SB.at[sl(o, xx, m4(a - 1), full, first[o])], RA[o].at[1, xx, :, lo[o]], s_r1, (*n, 3), minus),
            send(RB[o].at[xx, :, lo[o]], RA[o].at[0, xx, :, lo[o]], s_r1, (*n, 4), plus),
            send(RB[o].at[xx, :, hi[o]], RA[o].at[1, xx, :, hi[o]], s_r1, (*n, 5), minus)]

    hops = {(o, k): hop(o, k) for o in (1, 2) for k in range(4)}
    P2_1 = [[send(SB.at[xk[k], y, m4(z + j), whole[1]], RC1.at[j - 1, xk[k]], s_c1, (k, j - 1), along(2, j))
             for j in (2, 1, 3)] for k in range(4)]
    rel = (2, 1, 3)
    P3_1 = [send(SB.at[xk[k], y, z, whole[1]], RD.at[rel[k] - 1, whole[1]], s_rd, (1, rel[k] - 1), along(0, rel[k]))
            for k in range(3)]
    P2_2 = [send(SB.at[xk[k], :, z, whole[2]], RC2.at[rel[k] - 1], s_c2, (rel[k] - 1,), along(0, rel[k])) for k in range(3)]
    P3_2 = [send(SB.at[x, m4(y + j), z, whole[2]], RD.at[j - 1, whole[2]], s_rd, (2, j - 1), along(1, j)) for j in (2, 1, 3)]

    def start_hops(k):
        for n in range(4):
            for o in (1, 2):
                hops[o, k][n].start()

    def relay_hops(k):
        xx = xk[k]
        for o in (1, 2):
            for e in hops[o, k][:2]:
                e.wait_recv()

            def add(u, o=o):
                a = me[o]
                plus_into(RB[o], (xx, u, lo[o]), (SB, sl(o, xx, m4(a + 1), u, first[o])))
                plus_into(RB[o], (xx, u, hi[o]), (SB, sl(o, xx, m4(a - 1), u, second[o])))

            loop(4, add)
            for e in hops[o, k][4:]:
                e.start()

    def finish_hops(k):
        xx = xk[k]
        for o in (1, 2):
            for e in hops[o, k][2:]:
                e.wait_recv()

            def add(u, o=o):
                plus_into(SB, sl(o, xx, me[o], u, whole[o]), (RA[o], (0, xx, u)), (RA[o], (1, xx, u)))

            loop(4, add)
            for e in (P2_1[k] if o == 1 else P2_2[k:k + 1]):
                e.start()

    def finish_1(k):
        for e in P2_1[k]:
            e.wait_recv()
        plus_into(SB, (xk[k], y, z, whole[1]), *[(RC1, (j, xk[k])) for j in range(3)])
        if k < 3:
            P3_1[k].start()

    def relay_0(r):
        far0[r].wait_recv()
        rows, mine = ((lo, first), (hi, second))[r]

        def add(i):
            plus_into(RB0, (i // 4, i % 4, rows[0]), (SB, (xk[1 + r], i // 4, i % 4, mine[0])))

        loop(16, add)
        relay0[r].start()

    def gw_copy(n):
        m = (n + 4) % 7
        return pltpu.make_async_copy(stage.at[n % 2], gw_out.at[pl.ds(m * 512, 512)], s_out.at[n % 2])

    def gw(n):
        k = pl.ds((n + 4) % 7 * 512, 512)
        if n > 1:
            gw_copy(n - 2).wait()
        out = dot(H[:, :, :, :, k].reshape(1024, 512), T[:, :, :, :, cols_c].reshape(1024, C), ((0,), (0,)))
        out = out + dot(HO[:, :, :, :, k].reshape(1024, 512), GX[...].reshape(1024, C), ((0,), (0,)))
        stage[n % 2] = out.astype(BF)
        gw_copy(n).start()

    HXA = [send(H.at[xx, :, :, :, 2 * C:D], HO.at[xx, :, :, :, 2 * C:D], s_h, (0, xx), sibling) for xx in range(4)]
    HXB = [send(H.at[xx, :, :, :, 0:2 * C], HO.at[xx, :, :, :, 0:2 * C], s_h, (1, xx), sibling) for xx in range(4)]
    GXC = [send(T.at[xx, :, :, :, pl.ds(pl.multiple_of((1 - c) * C, C), C)], GX.at[xx], s_g, (k,), sibling)
           for k, xx in enumerate(xk)]
    cex = [[send(CT.at[a], CR.at[a, k], s_ct, (a, k), along(a, k + 1)) for k in range(3)] for a in range(3)]

    def sum_cross(a):
        for e in cex[a]:
            e.wait()
        CT[a + 1] = CT[a] + CR[a, 0] + CR[a, 1] + CR[a, 2]
        if a < 2:
            for e in cex[a + 1]:
                e.start()

    for k in range(4):
        for n in ((1, 4), (3, 6), (5, 2), (0,))[k]:
            A[n].wait_recv()
        if k == 3:
            local[5].wait()
        for q in range(2):
            grads(2 * xk[k] + q)
        units(xk[k])
        if k > 0:
            relay_hops(k - 1)
        start_hops(k)
        if k == 0:
            for e in far0:
                e.start()
        if k in (1, 2):
            near0[k - 1].start()
        GXC[k].start()
        if k == 1:
            for e in HXA:
                e.start()
        if k == 3:
            for e in A:
                e.wait_send()
            pl.semaphore_signal(s_free, inc=1, device_id=sibling, device_id_type=MESH)
        if k in (1, 2):
            relay_0(k - 1)
        if k > 2:
            finish_hops(k - 3)
    for e in cex[0]:
        e.start()
    pl.semaphore_wait(s_free, 1)
    for e in HXB:
        e.start()
    for e in GXC + HXA:
        e.wait_recv()
    gw(0)
    relay_hops(3)
    finish_hops(1)
    finish_1(0)
    for e in near0 + relay0:
        e.wait_recv()

    def add_0(i):
        plus_into(SB, (x, i // 4, i % 4, whole[0]), (RA0, (0, i // 4, i % 4)), (RA0, (1, i // 4, i % 4)))

    loop(16, add_0)
    for e in P2_0:
        e.start()
    gw(1)
    finish_hops(2)
    finish_1(1)
    sum_cross(0)
    gw(2)
    finish_hops(3)
    finish_1(2)
    sum_cross(1)
    for e in HXB:
        e.wait_recv()
    gw(3)
    finish_1(3)
    for e in P2_0 + P2_2:
        e.wait_recv()

    def add_1(u):
        plus_into(SB, (x, y, u, whole[0]), *[(RC0, (j, u)) for j in range(3)])
        plus_into(SB, (x, u, z, whole[2]), *[(RC2, (j, u)) for j in range(3)])

    loop(4, add_1)
    for e in P3_0 + P3_2:
        e.start()
    sum_cross(2)
    gw(4)
    gw(5)
    gw(6)
    b_me = x * 2 + p
    kl_out[...] = (CT[3, pl.ds(b_me, 1), :] - LSE[1, pl.ds(b_me, 1), :]) + LSE[0, pl.ds(b_me, 1), :]
    for e in P3_0 + P3_1 + P3_2:
        e.wait_recv()
    total = SB[x, y, z].astype(F32)
    for k in range(3):
        total = total + RD[k].astype(F32)
    gh_out[...] = total.astype(BF)

    for n in (5, 6):
        gw_copy(n).wait()
    for e in GXC + HXA + HXB:
        e.wait_send()
    for e in far0 + near0 + relay0 + P2_0 + P3_0 + P3_1 + P2_2 + P3_2:
        e.wait_send()
    for k in range(4):
        for e in hops[1, k] + hops[2, k] + P2_1[k]:
            e.wait_send()


def write_out(src, dst, held, sems):
    rows = [pl.ds(n * (D // 14), D // 14) for n in range(14)]
    into = [pltpu.make_async_copy(src.at[r], held.at[r], sems.at[0, n]) for n, r in enumerate(rows)]
    out = [pltpu.make_async_copy(held.at[r], dst.at[r], sems.at[1, n]) for n, r in enumerate(rows)]
    for e in into:
        e.start()
    for a, b in zip(into, out):
        a.wait()
        b.start()
    for e in out:
        e.wait()


def local(hidden, head_weight, teacher_logits, upstream):
    any_ = pl.BlockSpec(memory_space=pl.ANY)
    vmem = pl.BlockSpec(memory_space=pltpu.VMEM)
    dma = pltpu.SemaphoreType.DMA
    scratch = [
        pltpu.VMEM((4, 2, 4, 32, D), BF),
        pltpu.VMEM((4, 2, 4, 32, D), BF),
        pltpu.VMEM((D, 2 * C), BF),
        pltpu.VMEM((4, 2, 4, 32, 2 * C), BF),
        pltpu.VMEM((4, 2, 4, 32, 2 * C), F32),
        pltpu.VMEM((4, 2, 4, 32, C), BF),
        pltpu.VMEM((4, 4, 4, F, 128), BF),
        *[pltpu.VMEM((2, 4, 4, n, 128), BF) for n in COUNT],
        *[pltpu.VMEM((4, 4, n, 128), BF) for n in COUNT],
        *[pltpu.VMEM((3, 4, n, 128), BF) for n in COUNT],
        pltpu.VMEM((3, F, 128), BF),
        pltpu.VMEM((4, 2, 4, 32, 128), F32),
        pltpu.VMEM((4, 2, 4, 32, 128), F32),
        pltpu.VMEM((4, 4, 8, 128), F32),
        pltpu.VMEM((3, 3, 4, 8, 128), F32),
        pltpu.VMEM((4, 8, 128), F32),
        pltpu.VMEM((3, 3, 8, 128), F32),
        pltpu.VMEM((2, 8, 128), F32),
        pltpu.VMEM((4, 128, 128), F32),
        pltpu.VMEM((2, 512, C), BF),
        dma((6,)), dma((2,)), dma((2, 3)), dma((2, 4)), dma((2, 3)), dma((2, 4)), dma((2, 3, 2, 2)), dma((2, 3, 2, 2)),
        dma((2, 7)), dma((2,)), dma((2, 2, 4)), dma((2, 4)), dma((2, 3, 3)), dma((2, 3, 3)), dma((2, 6)), dma((2, 2, 4, 6)),
        dma((2, 3)), dma((2, 4, 3)), dma((2, 3)), dma((2, 3, 3)), dma((2,)), pltpu.SemaphoreType.REGULAR,
    ]
    gh, gw, kl = pl.pallas_call(
        kernel,
        out_shape=[jax.ShapeDtypeStruct((F, 128), BF), jax.ShapeDtypeStruct((D, C), BF),
                   jax.ShapeDtypeStruct((1, 128), F32)],
        in_specs=[any_, any_, any_, vmem],
        out_specs=[vmem, any_, vmem],
        scratch_shapes=scratch,
        compiler_params=pltpu.CompilerParams(collective_id=0, has_side_effects=True, vmem_limit_bytes=64 * 2**20 - 65536),
        cost_estimate=pl.CostEstimate(flops=45 * 10**9, bytes_accessed=60 * 2**20, transcendentals=8 * 2**20),
    )(hidden, head_weight, teacher_logits.reshape(2 * C, C), upstream.reshape(16, 128))
    gw = pl.pallas_call(
        write_out,
        out_shape=jax.ShapeDtypeStruct((D, C), BF),
        in_specs=[any_],
        out_specs=any_,
        scratch_shapes=[pltpu.VMEM((D, C), BF), dma((2, 14))],
        compiler_params=pltpu.CompilerParams(vmem_limit_bytes=60 * 2**20),
        cost_estimate=pl.CostEstimate(flops=0, bytes_accessed=14 * 2**20, transcendentals=0),
    )(gw)
    return gh.T, gw, kl.reshape(128)


def solution(mesh):
    return jax.shard_map(
        local,
        mesh=mesh,
        in_specs=(P("dp", None), P(None, ("dp", "vocab")), P("dp", None, "vocab"), P()),
        out_specs=(P("dp", "vocab"), P(None, ("dp", "vocab")), P("dp")),
        check_vma=False,
    )
```
